512 devices in a mesh: req: 8 (over x, core), pre: 64 (over y, z).
Axes of the slice: x: 4, y: 8, z: 8, core: 2. Of those that a mesh axis runs over, the one named last changes fastest.
Arguments:
- queries: bfloat16 [4, 64, 8192], P(None, 'req', 'pre')
- prefix_cache: bfloat16 [2, 32768, 1024], P(None, 'pre')
- suffix_pool: bfloat16 [2, 16384, 16, 1024], P(None, ('req', 'pre')), may hold values from -6 to 6
- suffix_lengths: int32 [64], P('req'), may hold values from 1 to 4092, 131072 in all
- page_table: int32 [64, 256], P('req'), may hold values from 0 to 16383, as said below
- out_weight: bfloat16 [8192, 8192], P('pre', 'req'), may hold values from -0.0625 to 0.0625
Outputs:
- attended: float32 [4, 64, 8192], P(None, 'req', 'pre')
- projected: float32 [256, 8192], P('pre', 'req')
The draws below stay inside these ranges and needn't reach their ends.
Inputs may be any that keep to these rules, and one draw needn't show every extreme that they name: Cached suffix tokens before the first new position; the keys of the 4 new positions sit at suffix tokens suffix_lengths[r] onward; some request has exactly 4092. `page_table`: the requests of aligned block b of 8 requests together hold each pool page b * 8 * 256 to (b + 1) * 8 * 256 - 1 exactly once.
All inputs are finite; a program needn't handle non-finite values. No bound on the sum of `suffix_lengths` on one device may be relied on, other than what follows from the above.
Results may differ from the reference program's by a relative error of at most 0.0075.
Values may be sent and summed in bfloat16 or wider, within the bound.
No kernel may reach another device: no remote copies, remote signals or barrier semaphores. Data moves between devices by JAX's collectives and lax.ppermute only.
A program may use at most 64 MiB of HBM per device.

```python
import math
import jax
import jax.numpy as jnp
import numpy as np
from jax import lax

H = 64
KVH = 8
HD = 128
D = 8192
STEPS = 4
PAGE = 16
PAGES_MAX = 256
REQ_DEV = 8
REQS = 64
PRE_LEN = 32768
SUF_MAX = 4096


def prefix_base(key):
    return jnp.clip(jax.random.normal(key, (2, PRE_LEN, KVH * HD), jnp.float32), -6.0, 6.0)


def draw_prefix_cache(key, part):
    drawn = prefix_base(key)
    return drawn.astype(jnp.bfloat16)


def draw_queries(key, part):
    key = jax.random.fold_in(key, 11)
    shape = (STEPS, REQS, H * HD)
    drawn = jnp.clip(jax.random.normal(key, shape, jnp.float32) * 2.5, -15.0, 15.0)
    return drawn.astype(jnp.bfloat16)


def draw_page_table(key, part):
    key = jax.random.fold_in(key, 13)
    blocks = REQS // REQ_DEV
    block_size = REQ_DEV * PAGES_MAX
    block_keys = jax.random.split(key, blocks)
    orders = jax.vmap(lambda block_key: jax.random.permutation(block_key, block_size))(block_keys)
    offsets = jnp.arange(blocks, dtype=jnp.int32)[:, None] * block_size
    return (orders.astype(jnp.int32) + offsets).reshape(REQS, PAGES_MAX)


def block_scale(key, shape, cuts, smallest, top_value):
    def one(axis_at, parts):
        heights = jax.random.uniform(jax.random.fold_in(jax.random.fold_in(key, 6), axis_at), (parts,), jnp.float32, smallest / len(cuts), top_value / len(cuts))
        return jnp.repeat(jnp.exp(heights), shape[axis_at] // parts).reshape((-1,) + (1,) * (len(shape) - axis_at - 1))

    loudness = one(*cuts[0])
    for cut in cuts[1:]:
        loudness = loudness * one(*cut)
    return loudness


def length_profile(number_of, total, bound, slope):
    weights = [(1 << 20) // math.isqrt(standing ** slope) + 1 for standing in range(2, number_of + 1)]
    surplus, given = total - bound - (number_of - 1), [1] * (number_of - 1)
    while surplus > 0:
        candidates = [i for i in range(number_of - 1) if given[i] < bound]
        pool, budget = sum([weights[i] for i in candidates]), surplus
        for i in candidates:
            addition = min(bound - given[i], max(1, budget * weights[i] // pool), surplus)
            given[i] = given[i] + addition
            surplus = surplus - addition
    return np.array([bound] + given)


def uneven(own_key, number_of, total, bound, skew):
    if number_of == 2:
        one = jax.random.randint(own_key, (), max(1, total - bound), min(bound, total - 1) + 1)
        return jnp.stack([one, total - one])
    tallies = jnp.asarray(length_profile(number_of, total, bound, skew), jnp.int32)
    twos = (number_of - 1) // 2
    donor, taker = tallies[1:1 + 2 * twos:2], tallies[2:2 + 2 * twos:2]
    slack = jnp.minimum(donor - 1, bound - taker)
    shifted = jax.random.randint(jax.random.fold_in(own_key, 1), (twos,), 0, 1 << 20) % (slack + 1)
    tallies = tallies.at[1:1 + 2 * twos:2].set(donor - shifted).at[2:2 + 2 * twos:2].set(taker + shifted)
    return tallies[jax.random.permutation(jax.random.fold_in(own_key, 2), number_of)]


def scatter_about(stream_key, extent, width, limit, shards=(), held_as=jnp.bfloat16):
    values = width * jax.random.normal(stream_key, extent, jnp.float32)
    if shards:
        values = values * block_scale(stream_key, extent, shards, -0.22, 0.18)
    return jnp.clip(values, -limit, limit).astype(held_as)


def setup_inputs(seed: int = 0) -> dict:
    streams_of = jax.random.split(jax.random.key(seed), 7)
    return {
        "queries": draw_queries(jax.random.fold_in(streams_of[6], 71), 0),
        "prefix_cache": draw_prefix_cache(jax.random.fold_in(streams_of[6], 71), 0),
        "suffix_pool": scatter_about(streams_of[2], (2, REQS * PAGES_MAX, PAGE, KVH * HD), 1.1, 6.0, ((1, 512),)),
        "suffix_lengths": uneven(streams_of[3], REQS, REQS * SUF_MAX // 2, SUF_MAX - STEPS, 2).astype(jnp.int32),
        "page_table": draw_page_table(jax.random.fold_in(streams_of[6], 71), 0),
        "out_weight": scatter_about(streams_of[5], (H * HD, D), (H * HD) ** -0.5, 0.0625, ((0, 64), (1, 8))),
    }


def reference(queries, prefix_cache, suffix_pool, suffix_lengths, page_table, out_weight):
    per_group = H // KVH
    scale_factor = 1.0 / math.sqrt(HD)
    prefix_keys = prefix_cache[0].reshape(PRE_LEN, KVH, HD)
    prefix_values = prefix_cache[1].reshape(PRE_LEN, KVH, HD)
    step_index = jnp.arange(STEPS, dtype=jnp.int32)
    token_index = jnp.arange(SUF_MAX, dtype=jnp.int32)
    prefix_seen = jnp.ones((STEPS, PRE_LEN), dtype=bool)

    def one_request(request):
        query_rows = lax.dynamic_index_in_dim(queries, request, 1, keepdims=False)
        query_tiles = query_rows.reshape(STEPS, KVH, per_group, HD).astype(jnp.float32)
        pages = lax.dynamic_index_in_dim(page_table, request, 0, keepdims=False).astype(jnp.int32)
        suffix_pages = jnp.take(suffix_pool, pages, axis=1)
        suffix_keys = suffix_pages[0].reshape(SUF_MAX, KVH, HD)
        suffix_values = suffix_pages[1].reshape(SUF_MAX, KVH, HD)
        all_keys = jnp.concatenate([prefix_keys, suffix_keys], 0).astype(jnp.float32)
        all_values = jnp.concatenate([prefix_values, suffix_values], 0).astype(jnp.float32)
        scores = jnp.einsum('sgxd,tgd->sgxt', query_tiles, all_keys) * scale_factor
        length = lax.dynamic_index_in_dim(suffix_lengths, request, 0, keepdims=False)
        seen = token_index[None, :] < (length + step_index + 1)[:, None]
        visible = jnp.concatenate([prefix_seen, seen], 1)[:, None, None, :]
        scores = jnp.where(visible, scores, -jnp.inf)
        row_max = lax.optimization_barrier(jnp.max(scores, axis=-1, keepdims=True))
        exps = jnp.exp(scores - row_max)
        weight_sum = lax.optimization_barrier(jnp.sum(exps, axis=-1))
        weights = lax.optimization_barrier(exps.astype(jnp.bfloat16)).astype(jnp.float32)
        numerator = jnp.einsum('sgxt,tgd->sgxd', weights, all_values)
        return (numerator / weight_sum[..., None]).reshape(STEPS, H * HD)
    stacked = lax.map(one_request, jnp.arange(REQS, dtype=jnp.int32))
    attended = jnp.transpose(stacked, (1, 0, 2))
    rounded = stacked.astype(jnp.bfloat16).reshape(REQS * STEPS, H * HD)
    projected = jnp.dot(rounded, out_weight, preferred_element_type=jnp.float32)
    return (attended, projected)
```

```python
import math

import jax
import jax.numpy as jnp
from jax import lax
from jax.sharding import PartitionSpec as P

H = 64
KVH = 8
HD = 128


def exchange(blocks, axis):
    return lax.all_to_all(blocks, axis, 0, 0, tiled=True)


def body(queries, prefix_cache, suffix_pool, suffix_lengths, page_table, out_weight):
    step_count, local_requests, _ = queries.shape
    rows = step_count * local_requests
    per_group = H // KVH
    holders = lax.axis_size("pre")
    members = lax.axis_size("req")
    own = jnp.transpose(queries, (1, 0, 2)).reshape(1, rows, HD)
    gathered = exchange(jnp.broadcast_to(own, (holders, rows, HD)), "pre")
    query_tiles = gathered.reshape(KVH, per_group * rows, HD)

    slot_count = suffix_pool.shape[1]
    page_length = suffix_pool.shape[2]
    suffix_tokens = slot_count * page_length
    prefix_tokens = prefix_cache.shape[1]
    first_slot = (lax.axis_index("req") * holders + lax.axis_index("pre")) * slot_count
    slot_ids = first_slot + jnp.arange(slot_count, dtype=jnp.int32)
    matches = page_table[:, :, None] == slot_ids[None, None, :]
    owned = jnp.any(matches, axis=1)
    page_rank = jnp.arange(page_table.shape[1], dtype=jnp.int32)
    page_number = jnp.sum(jnp.where(matches, page_rank[None, :, None], 0), axis=(0, 1))
    offsets = jnp.arange(page_length, dtype=jnp.int32)
    positions = (page_number[:, None] * page_length + offsets[None, :]).reshape(suffix_tokens)
    owned_tokens = jnp.repeat(owned, page_length, axis=1)
    limits = suffix_lengths[:, None] + jnp.arange(step_count, dtype=jnp.int32)[None, :] + 1
    seen = owned_tokens[:, None, :] & (positions[None, None, :] < limits[:, :, None])
    seen = seen.reshape(1, 1, rows, suffix_tokens)

    scale = 1.0 / math.sqrt(HD)

    def score(keys):
        tiles = keys.reshape(-1, KVH, HD)
        return scale * jnp.einsum("gmd,tgd->gmt", query_tiles, tiles, preferred_element_type=jnp.float32)

    prefix_scores = score(prefix_cache[0])
    suffix_scores = score(suffix_pool[0]).reshape(KVH, per_group, rows, suffix_tokens)
    suffix_scores = jnp.where(seen, suffix_scores, -jnp.inf).reshape(KVH, per_group * rows, suffix_tokens)
    row_max = jnp.maximum(jnp.max(prefix_scores, axis=-1), jnp.max(suffix_scores, axis=-1))
    prefix_exps = jnp.exp(prefix_scores - row_max[..., None])
    suffix_exps = jnp.exp(suffix_scores - row_max[..., None])
    weight_sum = jnp.sum(prefix_exps, axis=-1) + jnp.sum(suffix_exps, axis=-1)

    def weigh(exps, values):
        tiles = values.reshape(-1, KVH, HD)
        return jnp.einsum(
            "gmt,tgd->gmd", exps.astype(jnp.bfloat16), tiles, preferred_element_type=jnp.float32
        )

    numerator = weigh(prefix_exps, prefix_cache[1]) + weigh(suffix_exps, suffix_pool[1])
    share = (numerator / weight_sum[..., None]).astype(jnp.bfloat16).reshape(holders, rows, HD)
    log_total = (row_max + jnp.log(weight_sum)).reshape(holders, rows)
    high = lax.reduce_precision(log_total, 8, 7)
    rest = log_total - high
    middle = lax.reduce_precision(rest, 8, 7)
    stats = jnp.stack([high, middle, rest - middle], 1).astype(jnp.bfloat16)
    stats = jnp.pad(stats, ((0, 0), (0, 5), (0, HD - rows)))
    received = exchange(jnp.concatenate([share, stats], 1), "pre")
    shares = received[:, :rows].astype(jnp.float32)
    parts = received[:, rows : rows + 3, :rows].astype(jnp.float32)
    logs = parts[:, 0] + parts[:, 1] + parts[:, 2]
    factor = jnp.exp(logs - jnp.max(logs, axis=0))
    merged = jnp.sum(shares * factor[..., None], axis=0) / jnp.sum(factor, axis=0)[:, None]
    attended = jnp.transpose(merged.reshape(local_requests, step_count, HD), (1, 0, 2))

    rounded = merged.astype(jnp.bfloat16)
    flat_rows = exchange(jnp.broadcast_to(rounded[None], (members, rows, HD)), "req")
    flat_rows = flat_rows.reshape(members * rows, HD)
    partial = jnp.dot(flat_rows, out_weight, preferred_element_type=jnp.float32)
    columns = out_weight.shape[1] // HD
    blocks = partial.astype(jnp.bfloat16).reshape(holders, step_count, columns, HD)
    blocks = jnp.transpose(blocks, (0, 2, 1, 3)).reshape(holders, columns * step_count, HD)
    pieces = exchange(blocks, "pre")
    projected = jnp.sum(pieces.astype(jnp.float32), axis=0).reshape(columns, step_count, HD)
    projected = jnp.transpose(projected, (1, 0, 2)).reshape(step_count, columns * HD)
    return (attended, projected)


def solution(mesh):
    placed = (
        P(None, "req", "pre"),
        P(None, "pre", None),
        P(None, ("req", "pre"), None, None),
        P("req"),
        P("req", None),
        P("pre", "req"),
    )
    return jax.shard_map(
        body,
        mesh=mesh,
        in_specs=placed,
        out_specs=(P(None, "req", "pre"), P("pre", "req")),
        check_vma=False,
    )
```

```python
import math

import jax
import jax.numpy as jnp
from jax import lax
from jax.experimental import pallas as pl
from jax.experimental.pallas import tpu as pltpu
from jax.sharding import PartitionSpec as P

H = 64
KVH = 8
HD = 128
STAT_ROWS = 8
PRE = "pre"
MEGA = 1024 * 1024


def exchange(blocks, axis):
    return lax.all_to_all(blocks, axis, 0, 0, tiled=True)


def in_hbm(array):
    return pltpu.with_memory_space_constraint(array, pltpu.HBM)


def in_vmem(array):
    return pltpu.with_memory_space_constraint(array, pltpu.VMEM)


def spread_kernel(own_ref, out_ref):
    step_count, local_requests, _ = own_ref.shape
    own = own_ref[...].astype(jnp.float32)
    ordered = jnp.concatenate(
        [
            own[step, request : request + 1]
            for request in range(local_requests)
            for step in range(step_count)
        ],
        0,
    ).astype(out_ref.dtype)
    for holder in range(out_ref.shape[0]):
        out_ref[holder] = ordered


def spread(own, holders):
    rows = own.shape[0] * own.shape[1]
    return pl.pallas_call(
        spread_kernel,
        out_specs=pl.BlockSpec(memory_space=pltpu.VMEM),
        out_shape=pltpu.VMEM((holders, rows, HD), own.dtype),
        name="spread",
        compiler_params=pltpu.CompilerParams(vmem_limit_bytes=4 * MEGA),
    )(in_hbm(own))


def stage_kernel(prefix_ref, suffix_ref, keys_ref, sems):
    copies = [
        pltpu.make_async_copy(prefix_ref.at[0], keys_ref.at[0], sems.at[0]),
        pltpu.make_async_copy(suffix_ref.at[0], keys_ref.at[1], sems.at[1]),
    ]
    for copy in copies:
        copy.start()
    for copy in copies:
        copy.wait()


def stage(prefix_cache, suffix_cache):
    return pl.pallas_call(
        stage_kernel,
        in_specs=[pl.BlockSpec(memory_space=pl.ANY)] * 2,
        out_specs=pl.BlockSpec(memory_space=pltpu.VMEM),
        out_shape=pltpu.VMEM(prefix_cache.shape, prefix_cache.dtype),
        scratch_shapes=[pltpu.SemaphoreType.DMA((2,))],
        name="stage",
        compiler_params=pltpu.CompilerParams(vmem_limit_bytes=4 * MEGA),
        cost_estimate=pl.CostEstimate(flops=0, bytes_accessed=4 * MEGA, transcendentals=0),
    )(in_hbm(prefix_cache), in_hbm(suffix_cache))


def split(value):
    high = value.astype(jnp.bfloat16).astype(jnp.float32)
    rest = value - high
    middle = rest.astype(jnp.bfloat16).astype(jnp.float32)
    return high, middle, rest - middle


def attend_kernel(query_ref, keys_ref, prefix_hbm, suffix_hbm, mask_ref, out_ref, values_ref, sems):
    rows = query_ref.shape[1]
    per_group = H // KVH
    width = per_group * rows
    line = lax.broadcasted_iota(jnp.int32, (STAT_ROWS, width), 0)
    factor = math.log2(math.e) / math.sqrt(HD)
    suffix_tokens = mask_ref.shape[1]

    def lanes(group):
        return slice(group * HD, (group + 1) * HD)

    copies = []
    for group in range(KVH):
        part = pl.ds(group * HD, HD)
        for half, cache in enumerate((prefix_hbm, suffix_hbm)):
            copy = pltpu.make_async_copy(
                cache.at[1, :, part], values_ref.at[half, :, part], sems.at[half, group]
            )
            copy.start()
            copies.append(copy)

    def scores(group):
        query = query_ref[group * per_group : (group + 1) * per_group].reshape(width, HD)

        def score(keys):
            return lax.dot_general(query, keys, (((1,), (1,)), ((), ())), preferred_element_type=jnp.float32)

        prefix_scores = score(keys_ref[0, :, lanes(group)])
        suffix_scores = score(keys_ref[1, :, lanes(group)]).reshape(per_group, rows, suffix_tokens)
        return prefix_scores, (suffix_scores + mask_ref[...][None]).reshape(width, suffix_tokens)

    def weigh(group, prefix_scores, suffix_scores):
        row_max = jnp.maximum(
            jnp.max(prefix_scores, axis=1, keepdims=True), jnp.max(suffix_scores, axis=1, keepdims=True)
        )
        shift = row_max * factor
        prefix_exps = jnp.exp2(prefix_scores * factor - shift)
        suffix_exps = jnp.exp2(suffix_scores * factor - shift)
        total = jnp.sum(prefix_exps, axis=1, keepdims=True) + jnp.sum(suffix_exps, axis=1, keepdims=True)
        for half in range(2):
            copies[2 * group + half].wait()
        sums = jnp.dot(
            prefix_exps.astype(jnp.bfloat16), values_ref[0, :, lanes(group)], preferred_element_type=jnp.float32
        ) + jnp.dot(
            suffix_exps.astype(jnp.bfloat16), values_ref[1, :, lanes(group)], preferred_element_type=jnp.float32
        )
        share = sums * (1.0 / total)
        log_total = jnp.broadcast_to(shift + jnp.log2(total), (width, HD)).T[:STAT_ROWS]
        high, middle, low = split(log_total)
        stats = jnp.where(line == 0, high, jnp.where(line == 1, middle, jnp.where(line == 2, low, 0.0)))
        for head in range(per_group):
            first = head * rows
            tile = first // HD * HD
            stat = stats[:, tile : tile + HD]
            if first != tile:
                stat = pltpu.roll(stat, HD - (first - tile), 1)
            message = jnp.concatenate([share[first : first + rows], stat], 0)
            out_ref[group * per_group + head] = message.astype(jnp.bfloat16)

    held = scores(0)
    for group in range(KVH):
        following = scores(group + 1) if group + 1 < KVH else None
        weigh(group, *held)
        held = following


def attend(gathered, keys, prefix_cache, suffix_cache, mask):
    holders, rows, _ = gathered.shape
    tokens = prefix_cache.shape[1] + suffix_cache.shape[1]
    return pl.pallas_call(
        attend_kernel,
        in_specs=[
            pl.BlockSpec(memory_space=pltpu.VMEM),
            pl.BlockSpec(memory_space=pltpu.VMEM),
            pl.BlockSpec(memory_space=pltpu.HBM),
            pl.BlockSpec(memory_space=pltpu.HBM),
            pl.BlockSpec(memory_space=pltpu.VMEM),
        ],
        out_specs=pl.BlockSpec(memory_space=pltpu.VMEM),
        out_shape=jax.ShapeDtypeStruct((holders, rows + STAT_ROWS, HD), jnp.bfloat16),
        scratch_shapes=[
            pltpu.VMEM(suffix_cache.shape, suffix_cache.dtype),
            pltpu.SemaphoreType.DMA((2, KVH)),
        ],
        name="attend",
        compiler_params=pltpu.CompilerParams(vmem_limit_bytes=20 * MEGA),
        cost_estimate=pl.CostEstimate(
            flops=4 * H * rows * tokens * HD,
            bytes_accessed=5 * MEGA,
            transcendentals=H * rows * tokens,
        ),
    )(gathered, in_vmem(keys), in_hbm(prefix_cache), in_hbm(suffix_cache), mask)


def merge(received, rows):
    parts = received[:, rows : rows + 3, :rows].astype(jnp.float32)
    logs = parts[:, 0] + parts[:, 1] + parts[:, 2]
    factor = jnp.exp2(logs - jnp.max(logs, axis=0))
    merged = jnp.sum(received[:, :rows].astype(jnp.float32) * factor[..., None], axis=0)
    return merged / jnp.sum(factor, axis=0)[:, None]


def project_kernel(rows_ref, weight_ref, out_ref):
    steps = rows_ref.shape[0] // out_ref.shape[0]
    tile = 2 * steps
    pairs = rows_ref.shape[0] // tile
    columns = weight_ref.shape[1] // HD
    rows = rows_ref[...]
    lower = lax.broadcasted_iota(jnp.int32, (pairs, tile, HD), 1) < steps
    messages = [[], []]
    for pair in range(columns // 2):
        sums = jnp.dot(
            rows, weight_ref[:, pair * 2 * HD : (pair + 1) * 2 * HD], preferred_element_type=jnp.float32
        )
        even = sums[:, :HD].reshape(pairs, tile, HD)
        odd = sums[:, HD:].reshape(pairs, tile, HD)
        messages[0].append(jnp.where(lower, even, pltpu.roll(odd, steps, 1)))
        messages[1].append(jnp.where(lower, pltpu.roll(even, steps, 1), odd))
    for side in range(2):
        message = jnp.concatenate(messages[side], 1).astype(jnp.bfloat16)
        for pair in range(pairs):
            out_ref[pair * 2 + side] = message[pair]


def project(rows, weight, holders):
    lines = weight.shape[1] // HD * rows.shape[0] // holders
    return pl.pallas_call(
        project_kernel,
        out_shape=jax.ShapeDtypeStruct((holders, lines, HD), jnp.bfloat16),
        name="project",
        compiler_params=pltpu.CompilerParams(vmem_limit_bytes=16 * MEGA),
    )(rows, weight)


def suffix_mask(page_table, suffix_lengths, holder, slot_count, page_length, step_count):
    suffix_tokens = slot_count * page_length
    local_requests = page_table.shape[0]
    slot_ids = holder * slot_count + jnp.arange(slot_count, dtype=jnp.int32)
    matches = page_table[:, None, :] == slot_ids[None, :, None]
    ranks = jnp.arange(page_table.shape[1], dtype=jnp.int32) + 1
    held = jnp.max(jnp.where(matches, ranks, 0), axis=2)
    far = jnp.int32(1 << 30)
    starts = jnp.where(held > 0, (held - 1) * page_length, far)
    offsets = jnp.arange(page_length, dtype=jnp.int32)
    positions = (starts[:, :, None] + offsets).reshape(local_requests, 1, suffix_tokens)
    limits = suffix_lengths[:, None] + jnp.arange(step_count, dtype=jnp.int32)[None, :] + 1
    seen = positions < limits[:, :, None]
    mask = jnp.where(seen, 0.0, -jnp.inf).astype(jnp.float32)
    return mask.reshape(local_requests * step_count, suffix_tokens)


def body(queries, prefix_cache, suffix_pool, suffix_lengths, page_table, out_weight):
    step_count, local_requests, _ = queries.shape
    holders = lax.axis_size(PRE)
    gathered = exchange(spread(queries, holders), PRE)

    slot_count = suffix_pool.shape[1]
    page_length = suffix_pool.shape[2]
    holder = lax.axis_index("req") * holders + lax.axis_index(PRE)
    suffix_cache = suffix_pool.reshape(2, slot_count * page_length, KVH * HD)
    mask = suffix_mask(page_table, suffix_lengths, holder, slot_count, page_length, step_count)
    shares = attend(gathered, stage(prefix_cache, suffix_cache), prefix_cache, suffix_cache, mask)
    merged = merge(exchange(shares, PRE), step_count * local_requests)
    attended = jnp.transpose(merged.reshape(local_requests, step_count, HD), (1, 0, 2))
    copies = jnp.broadcast_to(merged.astype(jnp.bfloat16)[None], (lax.axis_size("req"),) + merged.shape)
    lines = exchange(copies, "req").reshape(-1, HD)
    pieces = exchange(project(lines, out_weight, holders), PRE)
    columns = out_weight.shape[1] // HD
    projected = jnp.sum(pieces.astype(jnp.float32), axis=0).reshape(columns, step_count, HD)
    projected = jnp.transpose(projected, (1, 0, 2)).reshape(step_count, columns * HD)
    return (attended, projected)


def solution(mesh):
    placed = (
        P(None, "req", PRE),
        P(None, PRE, None),
        P(None, ("req", PRE), None, None),
        P("req"),
        P("req", None),
        P(PRE, "req"),
    )
    return jax.shard_map(
        body,
        mesh=mesh,
        in_specs=placed,
        out_specs=(P(None, "req", PRE), P(PRE, "req")),
        check_vma=False,
    )
```

```python
import math

import jax
import jax.numpy as jnp
from jax import lax
from jax.experimental import pallas as pl
from jax.experimental.pallas import tpu as pltpu
from jax.sharding import Mesh
from jax.sharding import PartitionSpec as P

H = 64
KVH = 8
HD = 128
STAT_ROWS = 8
PRE = ("y", "zh", "zl")
MEGA = 1024 * 1024
EARLY = 2
LATE = ((2, 5), (5, 8))


def exchange(blocks, axis):
    return lax.all_to_all(blocks, axis, 0, 0, tiled=True)


def in_hbm(array):
    return pltpu.with_memory_space_constraint(array, pltpu.HBM)


def in_vmem(array):
    return pltpu.with_memory_space_constraint(array, pltpu.VMEM)


def spread_kernel(own_ref, out_ref):
    step_count, local_requests, _ = own_ref.shape
    own = own_ref[...].astype(jnp.float32)
    ordered = jnp.concatenate(
        [
            own[step, request : request + 1]
            for request in range(local_requests)
            for step in range(step_count)
        ],
        0,
    ).astype(out_ref.dtype)
    for holder in range(out_ref.shape[0]):
        out_ref[holder] = ordered


def spread(own, holders):
    rows = own.shape[0] * own.shape[1]
    return pl.pallas_call(
        spread_kernel,
        out_specs=pl.BlockSpec(memory_space=pltpu.VMEM),
        out_shape=pltpu.VMEM((holders, rows, HD), own.dtype),
        name="spread",
        compiler_params=pltpu.CompilerParams(vmem_limit_bytes=4 * MEGA),
    )(in_hbm(own))


def stage_kernel(prefix_ref, suffix_ref, keys_ref, values_ref, sems):
    lanes = pl.ds(0, values_ref.shape[2])
    copies = []
    for half, cache in enumerate((prefix_ref, suffix_ref)):
        copies.append(pltpu.make_async_copy(cache.at[0], keys_ref.at[half], sems.at[0, half]))
        copies.append(pltpu.make_async_copy(cache.at[1, :, lanes], values_ref.at[half], sems.at[1, half]))
    for copy in copies:
        copy.start()
    for copy in copies:
        copy.wait()


def stage(prefix_cache, suffix_cache):
    halves, tokens, _ = prefix_cache.shape
    return pl.pallas_call(
        stage_kernel,
        in_specs=[pl.BlockSpec(memory_space=pl.ANY)] * 2,
        out_specs=[pl.BlockSpec(memory_space=pltpu.VMEM)] * 2,
        out_shape=[
            pltpu.VMEM(prefix_cache.shape, prefix_cache.dtype),
            pltpu.VMEM((halves, tokens, EARLY * HD), prefix_cache.dtype),
        ],
        scratch_shapes=[pltpu.SemaphoreType.DMA((2, 2))],
        name="stage",
        compiler_params=pltpu.CompilerParams(vmem_limit_bytes=4 * MEGA),
        cost_estimate=pl.CostEstimate(flops=0, bytes_accessed=5 * MEGA, transcendentals=0),
    )(in_hbm(prefix_cache), in_hbm(suffix_cache))


def split(value):
    high = value.astype(jnp.bfloat16).astype(jnp.float32)
    rest = value - high
    middle = rest.astype(jnp.bfloat16).astype(jnp.float32)
    return high, middle, rest - middle


def attend_kernel(
    query_ref, keys_ref, early_ref, prefix_hbm, suffix_hbm, mask_ref, out_ref, values_ref, sems
):
    rows = query_ref.shape[1]
    per_group = H // KVH
    width = per_group * rows
    line = lax.broadcasted_iota(jnp.int32, (STAT_ROWS, width), 0)
    factor = math.log2(math.e) / math.sqrt(HD)
    suffix_tokens = mask_ref.shape[1]

    def lanes(group):
        return slice(group * HD, (group + 1) * HD)

    copies = {}
    for place, (first, last) in enumerate(LATE):
        part = pl.ds(first * HD, (last - first) * HD)
        copies[first] = [
            pltpu.make_async_copy(cache.at[1, :, part], values_ref.at[half, :, part], sems.at[half, place])
            for half, cache in enumerate((prefix_hbm, suffix_hbm))
        ]
        for copy in copies[first]:
            copy.start()

    def scores(group):
        query = query_ref[group * per_group : (group + 1) * per_group].reshape(width, HD)

        def score(keys):
            return lax.dot_general(query, keys, (((1,), (1,)), ((), ())), preferred_element_type=jnp.float32)

        prefix_scores = score(keys_ref[0, :, lanes(group)])
        suffix_scores = score(keys_ref[1, :, lanes(group)]).reshape(per_group, rows, suffix_tokens)
        return prefix_scores, (suffix_scores + mask_ref[...][None]).reshape(width, suffix_tokens)

    def weigh(group, prefix_scores, suffix_scores):
        row_max = jnp.maximum(
            jnp.max(prefix_scores, axis=1, keepdims=True), jnp.max(suffix_scores, axis=1, keepdims=True)
        )
        shift = row_max * factor
        prefix_exps = jnp.exp2(prefix_scores * factor - shift)
        suffix_exps = jnp.exp2(suffix_scores * factor - shift)
        total = jnp.sum(prefix_exps, axis=1, keepdims=True) + jnp.sum(suffix_exps, axis=1, keepdims=True)
        for copy in copies.get(group, ()):
            copy.wait()
        source = early_ref if group < EARLY else values_ref
        sums = jnp.dot(
            prefix_exps.astype(jnp.bfloat16), source[0, :, lanes(group)], preferred_element_type=jnp.float32
        ) + jnp.dot(
            suffix_exps.astype(jnp.bfloat16), source[1, :, lanes(group)], preferred_element_type=jnp.float32
        )
        share = sums * (1.0 / total)
        log_total = jnp.broadcast_to(shift + jnp.log2(total), (width, HD)).T[:STAT_ROWS]
        high, middle, low = split(log_total)
        stats = jnp.where(line == 0, high, jnp.where(line == 1, middle, jnp.where(line == 2, low, 0.0)))
        for head in range(per_group):
            first = head * rows
            tile = first // HD * HD
            stat = stats[:, tile : tile + HD]
            if first != tile:
                stat = pltpu.roll(stat, HD - (first - tile), 1)
            message = jnp.concatenate([share[first : first + rows], stat], 0)
            out_ref[group * per_group + head] = message.astype(jnp.bfloat16)

    held = scores(0)
    for group in range(KVH):
        following = scores(group + 1) if group + 1 < KVH else None
        weigh(group, *held)
        held = following


def attend(gathered, keys, early, prefix_cache, suffix_cache, mask):
    holders, rows, _ = gathered.shape
    tokens = prefix_cache.shape[1] + suffix_cache.shape[1]
    return pl.pallas_call(
        attend_kernel,
        in_specs=[
            pl.BlockSpec(memory_space=pltpu.VMEM),
            pl.BlockSpec(memory_space=pltpu.VMEM),
            pl.BlockSpec(memory_space=pltpu.VMEM),
            pl.BlockSpec(memory_space=pltpu.HBM),
            pl.BlockSpec(memory_space=pltpu.HBM),
            pl.BlockSpec(memory_space=pltpu.VMEM),
        ],
        out_specs=pl.BlockSpec(memory_space=pltpu.VMEM),
        out_shape=jax.ShapeDtypeStruct((holders, rows + STAT_ROWS, HD), jnp.bfloat16),
        scratch_shapes=[
            pltpu.VMEM(suffix_cache.shape, suffix_cache.dtype),
            pltpu.SemaphoreType.DMA((2, len(LATE))),
        ],
        name="attend",
        compiler_params=pltpu.CompilerParams(vmem_limit_bytes=20 * MEGA),
        cost_estimate=pl.CostEstimate(
            flops=4 * H * rows * tokens * HD,
            bytes_accessed=5 * MEGA,
            transcendentals=H * rows * tokens,
        ),
    )(gathered, in_vmem(keys), in_vmem(early), in_hbm(prefix_cache), in_hbm(suffix_cache), mask)


def merge(received, rows):
    parts = received[:, rows : rows + 3, :rows].astype(jnp.float32)
    logs = parts[:, 0] + parts[:, 1] + parts[:, 2]
    factor = jnp.exp2(logs - jnp.max(logs, axis=0))
    merged = jnp.sum(received[:, :rows].astype(jnp.float32) * factor[..., None], axis=0)
    return merged / jnp.sum(factor, axis=0)[:, None]


def project_kernel(place_ref, rows_ref, own_ref, other_ref, out_ref):
    groups, sides, lines, _ = rows_ref.shape
    steps = groups * lines // out_ref.shape[0]
    tile = 2 * steps
    pairs = groups * lines // tile
    columns = own_ref.shape[1] // HD
    first, second = rows_ref[:, 0].reshape(groups * lines, HD), rows_ref[:, 1].reshape(groups * lines, HD)
    here = jnp.full((groups * lines, HD), place_ref[0], jnp.int32) == 0
    first, second = first.astype(jnp.float32), second.astype(jnp.float32)
    rows = jnp.concatenate([jnp.where(here, first, second), jnp.where(here, second, first)], 1)
    rows = rows.astype(jnp.bfloat16)
    lower = lax.broadcasted_iota(jnp.int32, (pairs, tile, HD), 1) < steps
    messages = [[], []]
    for pair in range(columns // 2):
        part = slice(pair * 2 * HD, (pair + 1) * 2 * HD)
        weight = jnp.concatenate([own_ref[:, part], other_ref[:, part]], 0)
        sums = jnp.dot(rows, weight, preferred_element_type=jnp.float32)
        even = sums[:, :HD].reshape(pairs, tile, HD)
        odd = sums[:, HD:].reshape(pairs, tile, HD)
        messages[0].append(jnp.where(lower, even, pltpu.roll(odd, steps, 1)))
        messages[1].append(jnp.where(lower, pltpu.roll(even, steps, 1), odd))
    for side in range(2):
        message = jnp.concatenate(messages[side], 1).astype(jnp.bfloat16)
        for pair in range(pairs):
            out_ref[pair * 2 + side] = message[pair]


def project(rows, own, other, holders, place):
    groups, sides, lines, _ = rows.shape
    steps = groups * lines // holders
    return pl.pallas_call(
        project_kernel,
        in_specs=[pl.BlockSpec(memory_space=pltpu.SMEM)] + [pl.BlockSpec(memory_space=pltpu.VMEM)] * 3,
        out_shape=jax.ShapeDtypeStruct((holders, own.shape[1] // HD * steps, HD), jnp.bfloat16),
        name="project",
        compiler_params=pltpu.CompilerParams(vmem_limit_bytes=16 * MEGA),
    )(place, rows, own, other)


def suffix_mask(page_table, suffix_lengths, holder, slot_count, page_length, step_count):
    suffix_tokens = slot_count * page_length
    local_requests = page_table.shape[0]
    slot_ids = holder * slot_count + jnp.arange(slot_count, dtype=jnp.int32)
    matches = page_table[:, None, :] == slot_ids[None, :, None]
    ranks = jnp.arange(page_table.shape[1], dtype=jnp.int32) + 1
    held = jnp.max(jnp.where(matches, ranks, 0), axis=2)
    far = jnp.int32(1 << 30)
    starts = jnp.where(held > 0, (held - 1) * page_length, far)
    offsets = jnp.arange(page_length, dtype=jnp.int32)
    positions = (starts[:, :, None] + offsets).reshape(local_requests, 1, suffix_tokens)
    limits = suffix_lengths[:, None] + jnp.arange(step_count, dtype=jnp.int32)[None, :] + 1
    seen = positions < limits[:, :, None]
    mask = jnp.where(seen, 0.0, -jnp.inf).astype(jnp.float32)
    return mask.reshape(local_requests * step_count, suffix_tokens)


def body(queries, prefix_cache, suffix_pool, suffix_lengths, page_table, out_weight):
    step_count, local_requests, _ = queries.shape
    holders = lax.axis_size(PRE)
    outgoing = spread(queries, holders)
    gathered = exchange(outgoing, PRE)

    side = lax.axis_index("zl")
    width = out_weight.shape[1] // 2
    out_weight, outgoing = lax.optimization_barrier((out_weight, outgoing))
    own_half = lax.dynamic_slice_in_dim(out_weight, side * width, width, 1)
    other_half = lax.dynamic_slice_in_dim(out_weight, (1 - side) * width, width, 1)
    other_half = lax.ppermute(other_half, "zl", [(0, 1), (1, 0)])
    slot_count = suffix_pool.shape[1]
    page_length = suffix_pool.shape[2]
    holder = lax.axis_index("req") * holders + lax.axis_index(PRE)
    suffix_cache = suffix_pool.reshape(2, slot_count * page_length, KVH * HD)
    mask = suffix_mask(page_table, suffix_lengths, holder, slot_count, page_length, step_count)
    shares = attend(gathered, *stage(prefix_cache, suffix_cache), prefix_cache, suffix_cache, mask)
    shares, own_half, other_half = lax.optimization_barrier((shares, own_half, other_half))
    merged = merge(exchange(shares, PRE), step_count * local_requests)
    attended = jnp.transpose(merged.reshape(local_requests, step_count, HD), (1, 0, 2))
    members = lax.axis_size("req")
    copies = merged.astype(jnp.bfloat16)
    copies = jnp.broadcast_to(copies[None], (2 * members,) + copies.shape)
    lines = exchange(copies, ("req", "zl")).reshape((members, 2) + merged.shape)
    pieces = exchange(project(lines, own_half, other_half, holders, side.reshape(1)), PRE)
    sums = jnp.sum(pieces.astype(jnp.float32).reshape((-1, 2) + pieces.shape[1:]), axis=0)
    projected = jnp.transpose(sums.reshape(-1, step_count, HD), (1, 0, 2)).reshape(step_count, -1)
    return (attended, projected)


def solution(mesh):
    fine = Mesh(mesh.devices.reshape(mesh.shape["req"], 8, 4, 2), ("req",) + PRE)
    placed = (
        P(None, "req", PRE),
        P(None, PRE, None),
        P(None, ("req",) + PRE, None, None),
        P("req"),
        P("req", None),
        P(PRE, "req"),
    )
    return jax.shard_map(
        body,
        mesh=fine,
        in_specs=placed,
        out_specs=(P(None, "req", PRE), P(PRE, "req")),
        check_vma=False,
    )
```

```python
import math

import jax
import jax.numpy as jnp
from jax import lax
from jax.experimental import pallas as pl
from jax.experimental.pallas import tpu as pltpu
from jax.sharding import Mesh
from jax.sharding import PartitionSpec as P

H = 64
KVH = 8
HD = 128
STAT_ROWS = 8
SPARE = 2
PRE = ("y", "zh", "zl")
MEGA = 1024 * 1024
EARLY = 2
LATE = ((2, 5), (5, 8))


def exchange(blocks, axis):
    return lax.all_to_all(blocks, axis, 0, 0, tiled=True)


def in_hbm(array):
    return pltpu.with_memory_space_constraint(array, pltpu.HBM)


def in_vmem(array):
    return pltpu.with_memory_space_constraint(array, pltpu.VMEM)


def spread_kernel(own_ref, out_ref):
    step_count, local_requests, _ = own_ref.shape
    own = own_ref[...].astype(jnp.float32)
    ordered = jnp.concatenate(
        [
            own[step, request : request + 1]
            for request in range(local_requests)
            for step in range(step_count)
        ],
        0,
    ).astype(out_ref.dtype)
    for holder in range(out_ref.shape[0]):
        out_ref[holder] = ordered


def spread(own, holders):
    rows = own.shape[0] * own.shape[1]
    return pl.pallas_call(
        spread_kernel,
        out_specs=pl.BlockSpec(memory_space=pltpu.VMEM),
        out_shape=pltpu.VMEM((holders, rows, HD), own.dtype),
        name="spread",
        compiler_params=pltpu.CompilerParams(vmem_limit_bytes=4 * MEGA),
    )(own)


def stage_kernel(prefix_ref, suffix_ref, keys_ref, values_ref, sems):
    lanes = pl.ds(0, values_ref.shape[2])
    copies = []
    for half, cache in enumerate((prefix_ref, suffix_ref)):
        copies.append(pltpu.make_async_copy(cache.at[0], keys_ref.at[half], sems.at[0, half]))
        copies.append(pltpu.make_async_copy(cache.at[1, :, lanes], values_ref.at[half], sems.at[1, half]))
    for copy in copies:
        copy.start()
    for copy in copies:
        copy.wait()


def stage(prefix_cache, suffix_cache):
    halves, tokens, _ = prefix_cache.shape
    return pl.pallas_call(
        stage_kernel,
        in_specs=[pl.BlockSpec(memory_space=pl.ANY)] * 2,
        out_specs=[pl.BlockSpec(memory_space=pltpu.VMEM)] * 2,
        out_shape=[
            pltpu.VMEM(prefix_cache.shape, prefix_cache.dtype),
            pltpu.VMEM((halves, tokens, EARLY * HD), prefix_cache.dtype),
        ],
        scratch_shapes=[pltpu.SemaphoreType.DMA((2, 2))],
        name="stage",
        compiler_params=pltpu.CompilerParams(vmem_limit_bytes=4 * MEGA),
        cost_estimate=pl.CostEstimate(flops=0, bytes_accessed=5 * MEGA, transcendentals=0),
    )(in_hbm(prefix_cache), in_hbm(suffix_cache))


def split(value):
    high = value.astype(jnp.bfloat16).astype(jnp.float32)
    rest = value - high
    middle = rest.astype(jnp.bfloat16).astype(jnp.float32)
    return high, middle, rest - middle


def attend_kernel(
    query_ref, keys_ref, early_ref, prefix_hbm, suffix_hbm, mask_ref, out_ref, values_ref, sems
):
    rows = query_ref.shape[1]
    per_group = H // KVH
    width = per_group * rows
    lane_group = lax.broadcasted_iota(jnp.int32, (STAT_ROWS, HD), 1) // rows
    factor = math.log2(math.e) / math.sqrt(HD)
    suffix_tokens = mask_ref.shape[1]

    def lanes(group):
        return slice(group * HD, (group + 1) * HD)

    copies = {}
    for place, (first, last) in enumerate(LATE):
        part = pl.ds(first * HD, (last - first) * HD)
        copies[first] = [
            pltpu.make_async_copy(cache.at[1, :, part], values_ref.at[half, :, part], sems.at[half, place])
            for half, cache in enumerate((prefix_hbm, suffix_hbm))
        ]
        for copy in copies[first]:
            copy.start()

    def scores(group):
        query = query_ref[group * per_group : (group + 1) * per_group].reshape(width, HD)

        def score(keys):
            return lax.dot_general(query, keys, (((1,), (1,)), ((), ())), preferred_element_type=jnp.float32)

        prefix_scores = score(keys_ref[0, :, lanes(group)])
        suffix_scores = score(keys_ref[1, :, lanes(group)]).reshape(per_group, rows, suffix_tokens)
        return prefix_scores, (suffix_scores + mask_ref[...][None]).reshape(width, suffix_tokens)

    def weigh(group, prefix_scores, suffix_scores):
        row_max = jnp.maximum(
            jnp.max(prefix_scores, axis=1, keepdims=True), jnp.max(suffix_scores, axis=1, keepdims=True)
        )
        shift = row_max * factor
        prefix_exps = jnp.exp2(prefix_scores * factor - shift)
        suffix_exps = jnp.exp2(suffix_scores * factor - shift)
        total = jnp.sum(prefix_exps, axis=1, keepdims=True) + jnp.sum(suffix_exps, axis=1, keepdims=True)
        for copy in copies.get(group, ()):
            copy.wait()
        source = early_ref if group < EARLY else values_ref
        sums = jnp.dot(
            prefix_exps.astype(jnp.bfloat16), source[0, :, lanes(group)], preferred_element_type=jnp.float32
        ) + jnp.dot(
            suffix_exps.astype(jnp.bfloat16), source[1, :, lanes(group)], preferred_element_type=jnp.float32
        )
        share = sums * (1.0 / total)
        log_total = jnp.broadcast_to(shift + jnp.log2(total), (width, HD)).T[:STAT_ROWS]
        high, middle, low = split(log_total)
        pieces = []
        for head in range(per_group):
            first = head * rows
            tile = first // HD * HD
            stat = jnp.zeros((STAT_ROWS, HD), jnp.float32)
            for place, part in enumerate((high, middle, low)):
                turn = (place * rows + tile - first) % HD
                part = part[:, tile : tile + HD]
                stat = jnp.where(lane_group == place, pltpu.roll(part, turn, 1) if turn else part, stat)
            pieces += [share[first : first + rows], stat[:SPARE]]
        lines = per_group * (rows + SPARE)
        out_ref[group * lines : (group + 1) * lines] = jnp.concatenate(pieces, 0).astype(jnp.bfloat16)

    held = scores(0)
    for group in range(KVH):
        following = scores(group + 1) if group + 1 < KVH else None
        weigh(group, *held)
        held = following


def attend(gathered, keys, early, prefix_cache, suffix_cache, mask):
    holders, rows, _ = gathered.shape
    tokens = prefix_cache.shape[1] + suffix_cache.shape[1]
    return pl.pallas_call(
        attend_kernel,
        in_specs=[
            pl.BlockSpec(memory_space=pltpu.VMEM),
            pl.BlockSpec(memory_space=pltpu.VMEM),
            pl.BlockSpec(memory_space=pltpu.VMEM),
            pl.BlockSpec(memory_space=pltpu.HBM),
            pl.BlockSpec(memory_space=pltpu.HBM),
            pl.BlockSpec(memory_space=pltpu.VMEM),
        ],
        out_specs=pl.BlockSpec(memory_space=pltpu.VMEM),
        out_shape=jax.ShapeDtypeStruct((holders * (rows + SPARE), HD), jnp.bfloat16),
        scratch_shapes=[
            pltpu.VMEM(suffix_cache.shape, suffix_cache.dtype),
            pltpu.SemaphoreType.DMA((2, len(LATE))),
        ],
        name="attend",
        compiler_params=pltpu.CompilerParams(vmem_limit_bytes=20 * MEGA),
        cost_estimate=pl.CostEstimate(
            flops=4 * H * rows * tokens * HD,
            bytes_accessed=5 * MEGA,
            transcendentals=H * rows * tokens,
        ),
    )(gathered, in_vmem(keys), in_vmem(early), in_hbm(prefix_cache), in_hbm(suffix_cache), mask)


def merge_kernel(received_ref, merged_ref, copies_ref):
    rows = merged_ref.shape[0]
    lines = rows + SPARE
    holders = received_ref.shape[0] // lines
    tiles = received_ref.shape[0] // HD
    stats = []
    for holder in range(holders):
        place = holder * lines + rows
        base = place // 16 * 16
        stats.append(received_ref[base : base + 16].astype(jnp.float32)[place - base : place - base + 1])
    stats = jnp.concatenate(stats, 0)
    log_totals = stats + pltpu.roll(stats, HD - rows, 1) + pltpu.roll(stats, HD - 2 * rows, 1)
    factors = jnp.exp2(log_totals - jnp.max(log_totals, axis=0, keepdims=True))
    factors = factors * (1.0 / jnp.sum(factors, axis=0, keepdims=True))
    lane = lax.broadcasted_iota(jnp.int32, (STAT_ROWS, HD), 1)
    spans = [jnp.zeros((STAT_ROWS, HD), jnp.float32) for _ in range(tiles)]
    for holder in range(holders):
        tile, turn = divmod(holder * lines, HD)
        factor = jnp.broadcast_to(factors[holder : holder + 1], (STAT_ROWS, HD))
        if turn:
            factor = pltpu.roll(factor, turn, 1)
        spans[tile] = jnp.where((lane >= turn) & (lane < turn + rows), factor, spans[tile])
        if turn + rows > HD:
            spans[tile + 1] = jnp.where(lane < turn + rows - HD, factor, spans[tile + 1])
    row = lax.broadcasted_iota(jnp.int32, (rows, HD), 0)
    column = lax.broadcasted_iota(jnp.int32, (rows, HD), 1)
    weights = jnp.concatenate(
        [
            jnp.where(
                lax.rem(column + tile * HD, lines) == row, jnp.broadcast_to(spans[tile][:1], (rows, HD)), 0.0
            )
            for tile in range(tiles)
        ],
        1,
    )
    high = weights.astype(jnp.bfloat16)
    low = (weights - high.astype(jnp.float32)).astype(jnp.bfloat16)
    sums = jnp.dot(jnp.concatenate([high, low], 0), received_ref[...], preferred_element_type=jnp.float32)
    merged = sums[:rows] + sums[rows:]
    merged_ref[...] = merged
    rounded = merged.astype(jnp.bfloat16)
    for copy in range(copies_ref.shape[0]):
        copies_ref[copy] = rounded


def merge(received, rows, copies):
    return pl.pallas_call(
        merge_kernel,
        out_shape=[
            jax.ShapeDtypeStruct((rows, HD), jnp.float32),
            jax.ShapeDtypeStruct((copies, rows, HD), jnp.bfloat16),
        ],
        name="merge",
        compiler_params=pltpu.CompilerParams(vmem_limit_bytes=16 * MEGA),
    )(received)


def project_kernel(place_ref, rows_ref, own_ref, other_ref, out_ref):
    groups, sides, lines, _ = rows_ref.shape
    steps = groups * lines // out_ref.shape[0]
    tile = 2 * steps
    pairs = groups * lines // tile
    columns = own_ref.shape[1] // HD
    first, second = rows_ref[:, 0].reshape(groups * lines, HD), rows_ref[:, 1].reshape(groups * lines, HD)
    here = jnp.full((groups * lines, HD), place_ref[0], jnp.int32) == 0
    first, second = first.astype(jnp.float32), second.astype(jnp.float32)
    rows = jnp.concatenate([jnp.where(here, first, second), jnp.where(here, second, first)], 1)
    rows = rows.astype(jnp.bfloat16)
    lower = lax.broadcasted_iota(jnp.int32, (pairs, tile, HD), 1) < steps
    messages = [[], []]
    for pair in range(columns // 2):
        part = slice(pair * 2 * HD, (pair + 1) * 2 * HD)
        weight = jnp.concatenate([own_ref[:, part], other_ref[:, part]], 0)
        sums = jnp.dot(rows, weight, preferred_element_type=jnp.float32)
        even = sums[:, :HD].reshape(pairs, tile, HD)
        odd = sums[:, HD:].reshape(pairs, tile, HD)
        messages[0].append(jnp.where(lower, even, pltpu.roll(odd, steps, 1)))
        messages[1].append(jnp.where(lower, pltpu.roll(even, steps, 1), odd))
    for side in range(2):
        message = jnp.concatenate(messages[side], 1).astype(jnp.bfloat16)
        for pair in range(pairs):
            out_ref[pair * 2 + side] = message[pair]


def project(rows, own, other, holders, place):
    groups, sides, lines, _ = rows.shape
    steps = groups * lines // holders
    return pl.pallas_call(
        project_kernel,
        in_specs=[pl.BlockSpec(memory_space=pltpu.SMEM)] + [pl.BlockSpec(memory_space=pltpu.VMEM)] * 3,
        out_shape=jax.ShapeDtypeStruct((holders, own.shape[1] // HD * steps, HD), jnp.bfloat16),
        name="project",
        compiler_params=pltpu.CompilerParams(vmem_limit_bytes=16 * MEGA),
    )(place, rows, in_vmem(own), in_vmem(other))


def suffix_mask(page_table, suffix_lengths, holder, slot_count, page_length, step_count):
    suffix_tokens = slot_count * page_length
    local_requests = page_table.shape[0]
    slot_ids = holder * slot_count + jnp.arange(slot_count, dtype=jnp.int32)
    matches = page_table[:, None, :] == slot_ids[None, :, None]
    ranks = jnp.arange(page_table.shape[1], dtype=jnp.int32) + 1
    held = jnp.max(jnp.where(matches, ranks, 0), axis=2)
    far = jnp.int32(1 << 30)
    starts = jnp.where(held > 0, (held - 1) * page_length, far)
    offsets = jnp.arange(page_length, dtype=jnp.int32)
    positions = (starts[:, :, None] + offsets).reshape(local_requests, 1, suffix_tokens)
    limits = suffix_lengths[:, None] + jnp.arange(step_count, dtype=jnp.int32)[None, :] + 1
    seen = positions < limits[:, :, None]
    mask = jnp.where(seen, 0.0, -jnp.inf).astype(jnp.float32)
    return mask.reshape(local_requests * step_count, suffix_tokens)


def body(queries, prefix_cache, suffix_pool, suffix_lengths, page_table, out_weight):
    step_count, local_requests, _ = queries.shape
    holders = lax.axis_size(PRE)
    outgoing = spread(queries, holders)
    gathered = exchange(outgoing, PRE)

    side = lax.axis_index("zl")
    width = out_weight.shape[1] // 2
    out_weight, outgoing = lax.optimization_barrier((out_weight, outgoing))
    own_half = lax.dynamic_slice_in_dim(out_weight, side * width, width, 1)
    other_half = lax.dynamic_slice_in_dim(out_weight, (1 - side) * width, width, 1)
    other_half = lax.ppermute(other_half, "zl", [(0, 1), (1, 0)])
    slot_count = suffix_pool.shape[1]
    page_length = suffix_pool.shape[2]
    holder = lax.axis_index("req") * holders + lax.axis_index(PRE)
    suffix_cache = suffix_pool.reshape(2, slot_count * page_length, KVH * HD)
    mask = suffix_mask(page_table, suffix_lengths, holder, slot_count, page_length, step_count)
    shares = attend(gathered, *stage(prefix_cache, suffix_cache), prefix_cache, suffix_cache, mask)
    shares, own_half, other_half = lax.optimization_barrier((shares, own_half, other_half))
    rows = step_count * local_requests
    members = lax.axis_size("req")
    shape = shares.shape
    shares = exchange(shares.reshape(holders, -1, SPARE, HD), PRE).reshape(shape)
    merged, copies = merge(shares, rows, 2 * members)
    attended = jnp.transpose(merged.reshape(local_requests, step_count, HD), (1, 0, 2))
    lines = exchange(copies, ("req", "zl")).reshape((members, 2) + merged.shape)
    pieces = exchange(project(lines, own_half, other_half, holders, side.reshape(1)), PRE)
    sums = jnp.sum(pieces.astype(jnp.float32).reshape((-1, 2) + pieces.shape[1:]), axis=0)
    projected = jnp.transpose(sums.reshape(-1, step_count, HD), (1, 0, 2)).reshape(step_count, -1)
    return (attended, projected)


def solution(mesh):
    fine = Mesh(mesh.devices.reshape(mesh.shape["req"], 8, 4, 2), ("req",) + PRE)
    placed = (
        P(None, "req", PRE),
        P(None, PRE, None),
        P(None, ("req",) + PRE, None, None),
        P("req"),
        P("req", None),
        P(PRE, "req"),
    )
    return jax.shard_map(
        body,
        mesh=fine,
        in_specs=placed,
        out_specs=(P(None, "req", PRE), P(PRE, "req")),
        check_vma=False,
    )
```

```python
import math

import jax
import jax.numpy as jnp
from jax import lax
from jax.experimental import pallas as pl
from jax.experimental.pallas import tpu as pltpu
from jax.sharding import Mesh
from jax.sharding import PartitionSpec as P

H = 64
KVH = 8
HD = 128
STAT_ROWS = 8
SPARE = 2
PRE = ("y", "zh", "zl")
MEGA = 1024 * 1024
EARLY = 2
LATE = ((2, 5), (5, 8))


def exchange(blocks, axis):
    return lax.all_to_all(blocks, axis, 0, 0, tiled=True)


def in_hbm(array):
    return pltpu.with_memory_space_constraint(array, pltpu.HBM)


def in_vmem(array):
    return pltpu.with_memory_space_constraint(array, pltpu.VMEM)


def spread_kernel(own_ref, out_ref):
    step_count, local_requests, _ = own_ref.shape
    own = own_ref[...].astype(jnp.float32)
    ordered = jnp.concatenate(
        [
            own[step, request : request + 1]
            for request in range(local_requests)
            for step in range(step_count)
        ],
        0,
    ).astype(out_ref.dtype)
    for holder in range(out_ref.shape[0]):
        out_ref[holder] = ordered


def spread(own, holders):
    rows = own.shape[0] * own.shape[1]
    return pl.pallas_call(
        spread_kernel,
        out_specs=pl.BlockSpec(memory_space=pltpu.VMEM),
        out_shape=pltpu.VMEM((holders, rows, HD), own.dtype),
        name="spread",
        compiler_params=pltpu.CompilerParams(vmem_limit_bytes=4 * MEGA),
    )(own)


def stage_kernel(prefix_ref, suffix_ref, keys_ref, values_ref, sems):
    lanes = pl.ds(0, values_ref.shape[2])
    copies = []
    for half, cache in enumerate((prefix_ref, suffix_ref)):
        copies.append(pltpu.make_async_copy(cache.at[0], keys_ref.at[half], sems.at[0, half]))
        copies.append(pltpu.make_async_copy(cache.at[1, :, lanes], values_ref.at[half], sems.at[1, half]))
    for copy in copies:
        copy.start()
    for copy in copies:
        copy.wait()


def stage(prefix_cache, suffix_cache):
    halves, tokens, _ = prefix_cache.shape
    return pl.pallas_call(
        stage_kernel,
        in_specs=[pl.BlockSpec(memory_space=pl.ANY)] * 2,
        out_specs=[pl.BlockSpec(memory_space=pltpu.VMEM)] * 2,
        out_shape=[
            pltpu.VMEM(prefix_cache.shape, prefix_cache.dtype),
            pltpu.VMEM((halves, tokens, EARLY * HD), prefix_cache.dtype),
        ],
        scratch_shapes=[pltpu.SemaphoreType.DMA((2, 2))],
        name="stage",
        compiler_params=pltpu.CompilerParams(vmem_limit_bytes=4 * MEGA),
        cost_estimate=pl.CostEstimate(flops=0, bytes_accessed=5 * MEGA, transcendentals=0),
    )(in_hbm(prefix_cache), in_hbm(suffix_cache))


def split(value):
    high = value.astype(jnp.bfloat16).astype(jnp.float32)
    rest = value - high
    middle = rest.astype(jnp.bfloat16).astype(jnp.float32)
    return high, middle, rest - middle


def attend_kernel(
    query_ref, keys_ref, early_ref, prefix_hbm, suffix_hbm, mask_ref, out_ref, values_ref, sems
):
    rows = query_ref.shape[1]
    per_group = H // KVH
    width = per_group * rows
    lane_group = lax.broadcasted_iota(jnp.int32, (STAT_ROWS, HD), 1) // rows
    factor = math.log2(math.e) / math.sqrt(HD)
    suffix_tokens = mask_ref.shape[1]

    def lanes(group):
        return slice(group * HD, (group + 1) * HD)

    copies = {}
    for place, (first, last) in enumerate(LATE):
        part = pl.ds(first * HD, (last - first) * HD)
        copies[first] = [
            pltpu.make_async_copy(cache.at[1, :, part], values_ref.at[half, :, part], sems.at[half, place])
            for half, cache in enumerate((prefix_hbm, suffix_hbm))
        ]
        for copy in copies[first]:
            copy.start()

    def with_ones(values):
        return jnp.concatenate([values, jnp.ones(values.shape, values.dtype)], 1)

    def scores(group):
        query = query_ref[group * per_group : (group + 1) * per_group].reshape(width, HD)

        def score(keys):
            return lax.dot_general(query, keys, (((1,), (1,)), ((), ())), preferred_element_type=jnp.float32)

        prefix_scores = score(keys_ref[0, :, lanes(group)])
        suffix_scores = score(keys_ref[1, :, lanes(group)]).reshape(per_group, rows, suffix_tokens)
        return prefix_scores, (suffix_scores + mask_ref[...][None]).reshape(width, suffix_tokens)

    def weigh(group, prefix_scores, suffix_scores):
        row_max = jnp.maximum(
            jnp.max(prefix_scores, axis=1, keepdims=True), jnp.max(suffix_scores, axis=1, keepdims=True)
        )
        shift = row_max * factor
        prefix_exps = jnp.exp2(prefix_scores * factor - shift)
        suffix_exps = jnp.exp2(suffix_scores * factor - shift)
        for copy in copies.get(group, ()):
            copy.wait()
        source = early_ref if group < EARLY else values_ref
        sums = jnp.dot(
            prefix_exps.astype(jnp.bfloat16), with_ones(source[0, :, lanes(group)]), preferred_element_type=jnp.float32
        ) + jnp.dot(
            suffix_exps.astype(jnp.bfloat16), with_ones(source[1, :, lanes(group)]), preferred_element_type=jnp.float32
        )
        sums, total = sums[:, :HD], sums[:, HD:]
        share = sums * (1.0 / total)
        log_total = (shift + jnp.log2(total)).T[:STAT_ROWS]
        high, middle, low = split(log_total)
        pieces = []
        for head in range(per_group):
            first = head * rows
            tile = first // HD * HD
            stat = jnp.zeros((STAT_ROWS, HD), jnp.float32)
            for place, part in enumerate((high, middle, low)):
                turn = (place * rows + tile - first) % HD
                part = part[:, tile : tile + HD]
                stat = jnp.where(lane_group == place, pltpu.roll(part, turn, 1) if turn else part, stat)
            pieces += [share[first : first + rows], stat[:SPARE]]
        lines = per_group * (rows + SPARE)
        out_ref[group * lines : (group + 1) * lines] = jnp.concatenate(pieces, 0).astype(jnp.bfloat16)

    held = scores(0)
    for group in range(KVH):
        following = scores(group + 1) if group + 1 < KVH else None
        weigh(group, *held)
        held = following


def attend(gathered, keys, early, prefix_cache, suffix_cache, mask):
    holders, rows, _ = gathered.shape
    tokens = prefix_cache.shape[1] + suffix_cache.shape[1]
    return pl.pallas_call(
        attend_kernel,
        in_specs=[
            pl.BlockSpec(memory_space=pltpu.VMEM),
            pl.BlockSpec(memory_space=pltpu.VMEM),
            pl.BlockSpec(memory_space=pltpu.VMEM),
            pl.BlockSpec(memory_space=pltpu.HBM),
            pl.BlockSpec(memory_space=pltpu.HBM),
            pl.BlockSpec(memory_space=pltpu.VMEM),
        ],
        out_specs=pl.BlockSpec(memory_space=pltpu.VMEM),
        out_shape=jax.ShapeDtypeStruct((holders * (rows + SPARE), HD), jnp.bfloat16),
        scratch_shapes=[
            pltpu.VMEM(suffix_cache.shape, suffix_cache.dtype),
            pltpu.SemaphoreType.DMA((2, len(LATE))),
        ],
        name="attend",
        compiler_params=pltpu.CompilerParams(vmem_limit_bytes=20 * MEGA),
        cost_estimate=pl.CostEstimate(
            flops=4 * H * rows * tokens * HD,
            bytes_accessed=5 * MEGA,
            transcendentals=H * rows * tokens,
        ),
    )(gathered, in_vmem(keys), in_vmem(early), in_hbm(prefix_cache), in_hbm(suffix_cache), mask)


def merge_kernel(received_ref, merged_ref, copies_ref):
    rows = merged_ref.shape[0]
    lines = rows + SPARE
    holders = received_ref.shape[0] // lines
    tiles = received_ref.shape[0] // HD
    stats = []
    for holder in range(holders):
        place = holder * lines + rows
        base = place // 16 * 16
        stats.append(received_ref[base : base + 16].astype(jnp.float32)[place - base : place - base + 1])
    stats = jnp.concatenate(stats, 0)
    log_totals = stats + pltpu.roll(stats, HD - rows, 1) + pltpu.roll(stats, HD - 2 * rows, 1)
    factors = jnp.exp2(log_totals - jnp.max(log_totals, axis=0, keepdims=True))
    factors = factors * (1.0 / jnp.sum(factors, axis=0, keepdims=True))
    lane = lax.broadcasted_iota(jnp.int32, (STAT_ROWS, HD), 1)
    spans = [jnp.zeros((STAT_ROWS, HD), jnp.float32) for _ in range(tiles)]
    for holder in range(holders):
        tile, turn = divmod(holder * lines, HD)
        factor = jnp.broadcast_to(factors[holder : holder + 1], (STAT_ROWS, HD))
        if turn:
            factor = pltpu.roll(factor, turn, 1)
        spans[tile] = jnp.where((lane >= turn) & (lane < turn + rows), factor, spans[tile])
        if turn + rows > HD:
            spans[tile + 1] = jnp.where(lane < turn + rows - HD, factor, spans[tile + 1])
    row = lax.broadcasted_iota(jnp.int32, (rows, HD), 0)
    column = lax.broadcasted_iota(jnp.int32, (rows, HD), 1)
    weights = jnp.concatenate(
        [
            jnp.where(
                lax.rem(column + tile * HD, lines) == row, jnp.broadcast_to(spans[tile][:1], (rows, HD)), 0.0
            )
            for tile in range(tiles)
        ],
        1,
    )
    high = weights.astype(jnp.bfloat16)
    low = (weights - high.astype(jnp.float32)).astype(jnp.bfloat16)
    sums = jnp.dot(jnp.concatenate([high, low], 0), received_ref[...], preferred_element_type=jnp.float32)
    merged = sums[:rows] + sums[rows:]
    merged_ref[...] = merged
    rounded = merged.astype(jnp.bfloat16)
    for copy in range(copies_ref.shape[0]):
        copies_ref[copy] = rounded


def merge(received, rows, copies):
    return pl.pallas_call(
        merge_kernel,
        out_shape=[
            jax.ShapeDtypeStruct((rows, HD), jnp.float32),
            jax.ShapeDtypeStruct((copies, rows, HD), jnp.bfloat16),
        ],
        name="merge",
        compiler_params=pltpu.CompilerParams(vmem_limit_bytes=16 * MEGA),
    )(received)


def project_kernel(place_ref, rows_ref, own_ref, other_ref, out_ref):
    groups, sides, lines, _ = rows_ref.shape
    steps = groups * lines // out_ref.shape[0]
    tile = 2 * steps
    pairs = groups * lines // tile
    columns = own_ref.shape[1] // HD
    first, second = rows_ref[:, 0].reshape(groups * lines, HD), rows_ref[:, 1].reshape(groups * lines, HD)
    here = jnp.full((groups * lines, HD), place_ref[0], jnp.int32) == 0
    first, second = first.astype(jnp.float32), second.astype(jnp.float32)
    rows = jnp.concatenate([jnp.where(here, first, second), jnp.where(here, second, first)], 1)
    rows = rows.astype(jnp.bfloat16)
    lower = lax.broadcasted_iota(jnp.int32, (pairs, tile, HD), 1) < steps
    messages = [[], []]
    for pair in range(columns // 2):
        part = slice(pair * 2 * HD, (pair + 1) * 2 * HD)
        weight = jnp.concatenate([own_ref[:, part], other_ref[:, part]], 0)
        sums = jnp.dot(rows, weight, preferred_element_type=jnp.float32)
        even = sums[:, :HD].reshape(pairs, tile, HD)
        odd = sums[:, HD:].reshape(pairs, tile, HD)
        messages[0].append(jnp.where(lower, even, pltpu.roll(odd, steps, 1)))
        messages[1].append(jnp.where(lower, pltpu.roll(even, steps, 1), odd))
    for side in range(2):
        message = jnp.concatenate(messages[side], 1).astype(jnp.bfloat16)
        for pair in range(pairs):
            out_ref[pair * 2 + side] = message[pair]


def project(rows, own, other, holders, place):
    groups, sides, lines, _ = rows.shape
    steps = groups * lines // holders
    return pl.pallas_call(
        project_kernel,
        in_specs=[pl.BlockSpec(memory_space=pltpu.SMEM)] + [pl.BlockSpec(memory_space=pltpu.VMEM)] * 3,
        out_shape=jax.ShapeDtypeStruct((holders, own.shape[1] // HD * steps, HD), jnp.bfloat16),
        name="project",
        compiler_params=pltpu.CompilerParams(vmem_limit_bytes=16 * MEGA),
    )(place, rows, in_vmem(own), in_vmem(other))


def suffix_mask(page_table, suffix_lengths, holder, slot_count, page_length, step_count):
    suffix_tokens = slot_count * page_length
    local_requests = page_table.shape[0]
    slot_ids = holder * slot_count + jnp.arange(slot_count, dtype=jnp.int32)
    matches = page_table[:, None, :] == slot_ids[None, :, None]
    ranks = jnp.arange(page_table.shape[1], dtype=jnp.int32) + 1
    held = jnp.max(jnp.where(matches, ranks, 0), axis=2)
    far = jnp.int32(1 << 30)
    starts = jnp.where(held > 0, (held - 1) * page_length, far)
    offsets = jnp.arange(page_length, dtype=jnp.int32)
    positions = (starts[:, :, None] + offsets).reshape(local_requests, 1, suffix_tokens)
    limits = suffix_lengths[:, None] + jnp.arange(step_count, dtype=jnp.int32)[None, :] + 1
    seen = positions < limits[:, :, None]
    mask = jnp.where(seen, 0.0, -jnp.inf).astype(jnp.float32)
    return mask.reshape(local_requests * step_count, suffix_tokens)


def body(queries, prefix_cache, suffix_pool, suffix_lengths, page_table, out_weight):
    step_count, local_requests, _ = queries.shape
    holders = lax.axis_size(PRE)
    outgoing = spread(queries, holders)
    gathered = exchange(outgoing, PRE)

    side = lax.axis_index("zl")
    width = out_weight.shape[1] // 2
    out_weight, outgoing = lax.optimization_barrier((out_weight, outgoing))
    own_half = lax.dynamic_slice_in_dim(out_weight, side * width, width, 1)
    other_half = lax.dynamic_slice_in_dim(out_weight, (1 - side) * width, width, 1)
    other_half = lax.ppermute(other_half, "zl", [(0, 1), (1, 0)])
    slot_count = suffix_pool.shape[1]
    page_length = suffix_pool.shape[2]
    holder = lax.axis_index("req") * holders + lax.axis_index(PRE)
    suffix_cache = suffix_pool.reshape(2, slot_count * page_length, KVH * HD)
    mask = suffix_mask(page_table, suffix_lengths, holder, slot_count, page_length, step_count)
    shares = attend(gathered, *stage(prefix_cache, suffix_cache), prefix_cache, suffix_cache, mask)
    shares, own_half, other_half = lax.optimization_barrier((shares, own_half, other_half))
    rows = step_count * local_requests
    members = lax.axis_size("req")
    shape = shares.shape
    shares = exchange(shares.reshape(holders, -1, SPARE, HD), PRE).reshape(shape)
    merged, copies = merge(shares, rows, 2 * members)
    attended = jnp.transpose(merged.reshape(local_requests, step_count, HD), (1, 0, 2))
    lines = exchange(copies, ("req", "zl")).reshape((members, 2) + merged.shape)
    pieces = exchange(project(lines, own_half, other_half, holders, side.reshape(1)), PRE)
    sums = jnp.sum(pieces.astype(jnp.float32).reshape((-1, 2) + pieces.shape[1:]), axis=0)
    projected = jnp.transpose(sums.reshape(-1, step_count, HD), (1, 0, 2)).reshape(step_count, -1)
    return (attended, projected)


def solution(mesh):
    fine = Mesh(mesh.devices.reshape(mesh.shape["req"], 8, 4, 2), ("req",) + PRE)
    placed = (
        P(None, "req", PRE),
        P(None, PRE, None),
        P(None, ("req",) + PRE, None, None),
        P("req"),
        P("req", None),
        P(PRE, "req"),
    )
    return jax.shard_map(
        body,
        mesh=fine,
        in_specs=placed,
        out_specs=(P(None, "req", PRE), P(PRE, "req")),
        check_vma=False,
    )
```

```python
import math

import jax
import jax.numpy as jnp
from jax import lax
from jax.experimental import pallas as pl
from jax.experimental.pallas import tpu as pltpu
from jax.sharding import Mesh
from jax.sharding import PartitionSpec as P

H = 64
KVH = 8
HD = 128
STAT_ROWS = 8
SPARE = 2
PRE = ("y", "zh", "zl")
MEGA = 1024 * 1024
EARLY = 2
LATE = ((2, 5), (5, 8))


def exchange(blocks, axis):
    return lax.all_to_all(blocks, axis, 0, 0, tiled=True)


def in_hbm(array):
    return pltpu.with_memory_space_constraint(array, pltpu.HBM)


def in_vmem(array):
    return pltpu.with_memory_space_constraint(array, pltpu.VMEM)


def spread_kernel(own_ref, out_ref):
    step_count, local_requests, _ = own_ref.shape
    own = own_ref[...].astype(jnp.float32)
    ordered = jnp.concatenate(
        [
            own[step, request : request + 1]
            for request in range(local_requests)
            for step in range(step_count)
        ],
        0,
    ).astype(out_ref.dtype)
    for holder in range(out_ref.shape[0]):
        out_ref[holder] = ordered


def spread(own, holders):
    rows = own.shape[0] * own.shape[1]
    return pl.pallas_call(
        spread_kernel,
        out_specs=pl.BlockSpec(memory_space=pltpu.VMEM),
        out_shape=pltpu.VMEM((holders, rows, HD), own.dtype),
        name="spread",
        compiler_params=pltpu.CompilerParams(vmem_limit_bytes=4 * MEGA),
    )(own)


def stage_kernel(prefix_ref, suffix_ref, keys_ref, values_ref, sems):
    lanes = pl.ds(0, values_ref.shape[2])
    copies = []
    for half, cache in enumerate((prefix_ref, suffix_ref)):
        copies.append(pltpu.make_async_copy(cache.at[0], keys_ref.at[half], sems.at[0, half]))
        copies.append(pltpu.make_async_copy(cache.at[1, :, lanes], values_ref.at[half], sems.at[1, half]))
    for copy in copies:
        copy.start()
    for copy in copies:
        copy.wait()


def stage(prefix_cache, suffix_cache):
    halves, tokens, _ = prefix_cache.shape
    return pl.pallas_call(
        stage_kernel,
        in_specs=[pl.BlockSpec(memory_space=pl.ANY)] * 2,
        out_specs=[pl.BlockSpec(memory_space=pltpu.VMEM)] * 2,
        out_shape=[
            pltpu.VMEM(prefix_cache.shape, prefix_cache.dtype),
            pltpu.VMEM((halves, tokens, EARLY * HD), prefix_cache.dtype),
        ],
        scratch_shapes=[pltpu.SemaphoreType.DMA((2, 2))],
        name="stage",
        compiler_params=pltpu.CompilerParams(vmem_limit_bytes=4 * MEGA),
        cost_estimate=pl.CostEstimate(flops=0, bytes_accessed=5 * MEGA, transcendentals=0),
    )(in_hbm(prefix_cache), in_hbm(suffix_cache))


def split(value):
    high = value.astype(jnp.bfloat16).astype(jnp.float32)
    rest = value - high
    middle = rest.astype(jnp.bfloat16).astype(jnp.float32)
    return high, middle, rest - middle


def attend_kernel(
    query_ref, keys_ref, early_ref, prefix_hbm, suffix_hbm, mask_ref, out_ref, values_ref, sems
):
    rows = query_ref.shape[1]
    per_group = H // KVH
    width = per_group * rows
    lane_group = lax.broadcasted_iota(jnp.int32, (STAT_ROWS, HD), 1) // rows
    factor = math.log2(math.e) / math.sqrt(HD)
    suffix_tokens = mask_ref.shape[1]

    def lanes(group):
        return slice(group * HD, (group + 1) * HD)

    copies = {}
    for place, (first, last) in enumerate(LATE):
        part = pl.ds(first * HD, (last - first) * HD)
        copies[first] = [
            pltpu.make_async_copy(cache.at[1, :, part], values_ref.at[half, :, part], sems.at[half, place])
            for half, cache in enumerate((prefix_hbm, suffix_hbm))
        ]
        for copy in copies[first]:
            copy.start()

    def with_ones(values):
        return jnp.concatenate([values, jnp.ones(values.shape, values.dtype)], 1)

    def scores(group):
        query = query_ref[group * per_group : (group + 1) * per_group].reshape(width, HD)

        def score(keys):
            return lax.dot_general(query, keys, (((1,), (1,)), ((), ())), preferred_element_type=jnp.float32)

        prefix_scores = score(keys_ref[0, :, lanes(group)])
        suffix_scores = score(keys_ref[1, :, lanes(group)]).reshape(per_group, rows, suffix_tokens)
        return prefix_scores, (suffix_scores + mask_ref[...][None]).reshape(width, suffix_tokens)

    def weigh(group, prefix_scores, suffix_scores):
        row_max = jnp.maximum(
            jnp.max(prefix_scores, axis=1, keepdims=True), jnp.max(suffix_scores, axis=1, keepdims=True)
        )
        shift = row_max * factor
        prefix_exps = jnp.exp2(prefix_scores * factor - shift)
        suffix_exps = jnp.exp2(suffix_scores * factor - shift)
        for copy in copies.get(group, ()):
            copy.wait()
        source = early_ref if group < EARLY else values_ref
        sums = jnp.dot(
            prefix_exps.astype(jnp.bfloat16), with_ones(source[0, :, lanes(group)]), preferred_element_type=jnp.float32
        ) + jnp.dot(
            suffix_exps.astype(jnp.bfloat16), with_ones(source[1, :, lanes(group)]), preferred_element_type=jnp.float32
        )
        sums, total = sums[:, :HD], sums[:, HD:]
        share = sums * (1.0 / total)
        log_total = (shift + jnp.log2(total)).T[:STAT_ROWS]
        high, middle, low = split(log_total)
        pieces = []
        for head in range(per_group):
            first = head * rows
            tile = first // HD * HD
            stat = jnp.zeros((STAT_ROWS, HD), jnp.float32)
            for place, part in enumerate((high, middle, low)):
                turn = (place * rows + tile - first) % HD
                part = part[:, tile : tile + HD]
                stat = jnp.where(lane_group == place, pltpu.roll(part, turn, 1) if turn else part, stat)
            pieces += [share[first : first + rows], stat[:SPARE]]
        lines = per_group * (rows + SPARE)
        out_ref[group * lines : (group + 1) * lines] = jnp.concatenate(pieces, 0).astype(jnp.bfloat16)

    held = scores(0)
    for group in range(KVH):
        following = scores(group + 1) if group + 1 < KVH else None
        weigh(group, *held)
        held = following


def attend(gathered, keys, early, prefix_cache, suffix_cache, mask):
    holders, rows, _ = gathered.shape
    tokens = prefix_cache.shape[1] + suffix_cache.shape[1]
    return pl.pallas_call(
        attend_kernel,
        in_specs=[
            pl.BlockSpec(memory_space=pltpu.VMEM),
            pl.BlockSpec(memory_space=pltpu.VMEM),
            pl.BlockSpec(memory_space=pltpu.VMEM),
            pl.BlockSpec(memory_space=pltpu.HBM),
            pl.BlockSpec(memory_space=pltpu.HBM),
            pl.BlockSpec(memory_space=pltpu.VMEM),
        ],
        out_specs=pl.BlockSpec(memory_space=pltpu.VMEM),
        out_shape=jax.ShapeDtypeStruct((holders * (rows + SPARE), HD), jnp.bfloat16),
        scratch_shapes=[
            pltpu.VMEM(suffix_cache.shape, suffix_cache.dtype),
            pltpu.SemaphoreType.DMA((2, len(LATE))),
        ],
        name="attend",
        compiler_params=pltpu.CompilerParams(vmem_limit_bytes=20 * MEGA),
        cost_estimate=pl.CostEstimate(
            flops=4 * H * rows * tokens * HD,
            bytes_accessed=5 * MEGA,
            transcendentals=H * rows * tokens,
        ),
    )(gathered, in_vmem(keys), in_vmem(early), in_hbm(prefix_cache), in_hbm(suffix_cache), mask)


def merge_kernel(received_ref, attended_ref, copies_ref):
    steps, requests, _ = attended_ref.shape
    rows = steps * requests
    lines = rows + SPARE
    holders = received_ref.shape[0] // lines
    tiles = received_ref.shape[0] // HD
    stats = []
    for holder in range(holders):
        place = holder * lines + rows
        base = place // 16 * 16
        stats.append(received_ref[base : base + 16].astype(jnp.float32)[place - base : place - base + 1])
    stats = jnp.concatenate(stats, 0)
    log_totals = stats + pltpu.roll(stats, HD - rows, 1) + pltpu.roll(stats, HD - 2 * rows, 1)
    factors = jnp.exp2(log_totals - jnp.max(log_totals, axis=0, keepdims=True))
    factors = factors * (1.0 / jnp.sum(factors, axis=0, keepdims=True))
    lane = lax.broadcasted_iota(jnp.int32, (STAT_ROWS, HD), 1)
    spans = [jnp.zeros((STAT_ROWS, HD), jnp.float32) for _ in range(tiles)]
    for holder in range(holders):
        tile, turn = divmod(holder * lines, HD)
        factor = jnp.broadcast_to(factors[holder : holder + 1], (STAT_ROWS, HD))
        if turn:
            factor = pltpu.roll(factor, turn, 1)
        spans[tile] = jnp.where((lane >= turn) & (lane < turn + rows), factor, spans[tile])
        if turn + rows > HD:
            spans[tile + 1] = jnp.where(lane < turn + rows - HD, factor, spans[tile + 1])
    row = lax.broadcasted_iota(jnp.int32, (rows, HD), 0)
    column = lax.broadcasted_iota(jnp.int32, (rows, HD), 1)
    weights = jnp.concatenate(
        [
            jnp.where(
                lax.rem(column + tile * HD, lines) == row, jnp.broadcast_to(spans[tile][:1], (rows, HD)), 0.0
            )
            for tile in range(tiles)
        ],
        1,
    )
    high = weights.astype(jnp.bfloat16)
    low = (weights - high.astype(jnp.float32)).astype(jnp.bfloat16)
    sums = jnp.dot(jnp.concatenate([high, low], 0), received_ref[...], preferred_element_type=jnp.float32)
    merged = sums[:rows] + sums[rows:]
    by_step = [
        merged[request * steps + step : request * steps + step + 1]
        for step in range(steps)
        for request in range(requests)
    ]
    attended_ref[...] = jnp.concatenate(by_step, 0).reshape(steps, requests, HD)
    rounded = merged.astype(jnp.bfloat16)
    for copy in range(copies_ref.shape[0]):
        copies_ref[copy] = rounded


def merge(received, steps, requests, copies):
    return pl.pallas_call(
        merge_kernel,
        out_shape=[
            jax.ShapeDtypeStruct((steps, requests, HD), jnp.float32),
            jax.ShapeDtypeStruct((copies, steps * requests, HD), jnp.bfloat16),
        ],
        name="merge",
        compiler_params=pltpu.CompilerParams(vmem_limit_bytes=16 * MEGA),
    )(received)


def project_kernel(place_ref, rows_ref, own_ref, other_ref, out_ref):
    groups, sides, lines, _ = rows_ref.shape
    steps = groups * lines // out_ref.shape[0]
    tile = 2 * steps
    pairs = groups * lines // tile
    columns = own_ref.shape[1] // HD
    first, second = rows_ref[:, 0].reshape(groups * lines, HD), rows_ref[:, 1].reshape(groups * lines, HD)
    here = jnp.full((groups * lines, HD), place_ref[0], jnp.int32) == 0
    first, second = first.astype(jnp.float32), second.astype(jnp.float32)
    rows = jnp.concatenate([jnp.where(here, first, second), jnp.where(here, second, first)], 1)
    rows = rows.astype(jnp.bfloat16)
    lower = lax.broadcasted_iota(jnp.int32, (pairs, tile, HD), 1) < steps
    messages = [[], []]
    for pair in range(columns // 2):
        part = slice(pair * 2 * HD, (pair + 1) * 2 * HD)
        weight = jnp.concatenate([own_ref[:, part], other_ref[:, part]], 0)
        sums = jnp.dot(rows, weight, preferred_element_type=jnp.float32)
        even = sums[:, :HD].reshape(pairs, tile, HD)
        odd = sums[:, HD:].reshape(pairs, tile, HD)
        messages[0].append(jnp.where(lower, even, pltpu.roll(odd, steps, 1)))
        messages[1].append(jnp.where(lower, pltpu.roll(even, steps, 1), odd))
    for side in range(2):
        message = jnp.concatenate(messages[side], 1).astype(jnp.bfloat16)
        for pair in range(pairs):
            out_ref[pair * 2 + side] = message[pair]


def project(rows, own, other, holders, place):
    groups, sides, lines, _ = rows.shape
    steps = groups * lines // holders
    return pl.pallas_call(
        project_kernel,
        in_specs=[pl.BlockSpec(memory_space=pltpu.SMEM)] + [pl.BlockSpec(memory_space=pltpu.VMEM)] * 3,
        out_shape=jax.ShapeDtypeStruct((holders, own.shape[1] // HD * steps, HD), jnp.bfloat16),
        name="project",
        compiler_params=pltpu.CompilerParams(vmem_limit_bytes=16 * MEGA),
    )(place, rows, in_vmem(own), in_vmem(other))


def suffix_mask(page_table, suffix_lengths, holder, slot_count, page_length, step_count):
    suffix_tokens = slot_count * page_length
    local_requests = page_table.shape[0]
    slot_ids = holder * slot_count + jnp.arange(slot_count, dtype=jnp.int32)
    matches = page_table[:, None, :] == slot_ids[None, :, None]
    ranks = jnp.arange(page_table.shape[1], dtype=jnp.int32) + 1
    held = jnp.max(jnp.where(matches, ranks, 0), axis=2)
    far = jnp.int32(1 << 30)
    starts = jnp.where(held > 0, (held - 1) * page_length, far)
    offsets = jnp.arange(page_length, dtype=jnp.int32)
    positions = (starts[:, :, None] + offsets).reshape(local_requests, 1, suffix_tokens)
    limits = suffix_lengths[:, None] + jnp.arange(step_count, dtype=jnp.int32)[None, :] + 1
    seen = positions < limits[:, :, None]
    mask = jnp.where(seen, 0.0, -jnp.inf).astype(jnp.float32)
    return mask.reshape(local_requests * step_count, suffix_tokens)


def body(queries, prefix_cache, suffix_pool, suffix_lengths, page_table, out_weight):
    step_count, local_requests, _ = queries.shape
    holders = lax.axis_size(PRE)
    outgoing = spread(queries, holders)
    gathered = exchange(outgoing, PRE)

    side = lax.axis_index("zl")
    width = out_weight.shape[1] // 2
    out_weight, outgoing = lax.optimization_barrier((out_weight, outgoing))
    own_half = lax.dynamic_slice_in_dim(out_weight, side * width, width, 1)
    other_half = lax.dynamic_slice_in_dim(out_weight, (1 - side) * width, width, 1)
    other_half = lax.ppermute(other_half, "zl", [(0, 1), (1, 0)])
    slot_count = suffix_pool.shape[1]
    page_length = suffix_pool.shape[2]
    holder = lax.axis_index("req") * holders + lax.axis_index(PRE)
    suffix_cache = suffix_pool.reshape(2, slot_count * page_length, KVH * HD)
    mask = suffix_mask(page_table, suffix_lengths, holder, slot_count, page_length, step_count)
    shares = attend(gathered, *stage(prefix_cache, suffix_cache), prefix_cache, suffix_cache, mask)
    shares, own_half, other_half = lax.optimization_barrier((shares, own_half, other_half))
    members = lax.axis_size("req")
    shape = shares.shape
    shares = exchange(shares.reshape(holders, -1, SPARE, HD), PRE).reshape(shape)
    attended, copies = merge(shares, step_count, local_requests, 2 * members)
    lines = exchange(copies, ("req", "zl")).reshape((members, 2) + copies.shape[1:])
    pieces = exchange(project(lines, own_half, other_half, holders, side.reshape(1)), PRE)
    sums = jnp.sum(pieces.astype(jnp.float32).reshape((-1, 2) + pieces.shape[1:]), axis=0)
    projected = jnp.transpose(sums.reshape(-1, step_count, HD), (1, 0, 2)).reshape(step_count, -1)
    return (attended, projected)


def solution(mesh):
    fine = Mesh(mesh.devices.reshape(mesh.shape["req"], 8, 4, 2), ("req",) + PRE)
    placed = (
        P(None, "req", PRE),
        P(None, PRE, None),
        P(None, ("req",) + PRE, None, None),
        P("req"),
        P("req", None),
        P(PRE, "req"),
    )
    return jax.shard_map(
        body,
        mesh=fine,
        in_specs=placed,
        out_specs=(P(None, "req", PRE), P(PRE, "req")),
        check_vma=False,
    )
```
